256 devices in a mesh: row: 4 (over x), col: 16 (over y_lo, z), rep: 4 (over y_hi, core).
Axes of the slice: x: 4, y: 4 (y_hi: 2, y_lo: 2; y = y_hi * 2 + y_lo), z: 8, core: 2. Of those that a mesh axis runs over, the one named last changes fastest.
Arguments:
- a_vals: float32 [96, 12, 128, 128], P('col', 'row'), may hold values from -6 to 6
- a_group: int32 [96, 12, 1], P('col', 'row'), may hold values from 0 to 63; in each aligned block of 72 rows (0 to 71, 72 to 143, ..., all dimensions but the last counted through in order) at most 2 rows name the same one
- a_offset: int32 [96, 12], P('col', 'row'), may hold values from 0 to 4
- b_vals: float32 [320, 4, 3, 128, 128], P(('col', 'rep'), 'row'), may hold values from -0.5 to 0.5
- b_cols: int32 [320, 4, 3], P(('col', 'rep'), 'row'), may hold values from 0 to 15
- c_cols: int32 [96, 4, 4], P('col', 'row'), may hold values from 0 to 15, as said below
Outputs:
- c_vals: float32 [96, 4, 4, 128, 128], P('col', 'row', 'rep')
The draws below stay inside these ranges and needn't reach their ends.
Inputs may be any that keep to these rules, and one draw needn't show every extreme that they name: `a_group`: among the 72 stored A blocks of each aligned set of 6 block rows, at most 2 share one group, and 2 is reached. The 4 entries of c_cols[i, r] are distinct.
All inputs are finite; a program needn't handle non-finite values.
Results may differ from the reference program's by a relative error of at most 0.0003.
Values sent between devices are 32-bit elements; how exact they have to be, the bound alone decides.
A program may use at most 192 MiB of HBM per device.

```python
import math
import jax
import jax.numpy as jnp
import numpy as np
from jax import lax

BS = 128
KA = 12
KBG = 3
KCG = 4
JG = 16
RB = 6
KPG = 5
NBR = 96
GROUPS = 64
NKB = 320
CAP = 2
N_ROW = 4


def draw_c_cols(key, part):
    key = jax.random.fold_in(key, 7)
    scores = jax.random.randint(key, (NBR, N_ROW, JG), 0, 2 ** 20) * JG + jnp.arange(JG, dtype=jnp.int32)
    ordered = jnp.argsort(scores, axis=-1)
    return ordered[:, :, :KCG].astype(jnp.int32)


def touch_ends(array, stream_key, smallest, high):
    shape = array.shape
    spot = [jax.random.randint(jax.random.fold_in(stream_key, axis), (), 0, shape[axis]) for axis in range(len(shape))]
    array = array.at[tuple(spot)].set(smallest)
    longest = shape.index(max(shape))
    spot[longest] = (spot[longest] + 1) % shape[longest]
    return array.at[tuple(spot)].set(high)


def block_levels(own_key, extent, shards, smallest, largest):
    loudness = 1.0
    for dim, blocks in shards:
        draws = jax.random.uniform(jax.random.fold_in(jax.random.fold_in(own_key, 6), dim), (blocks,), jnp.float32, smallest / len(shards), largest / len(shards))
        loudness = loudness * jnp.repeat(jnp.exp(draws), extent[dim] // blocks).reshape((-1,) + (1,) * (len(extent) - 1 - dim))
    return loudness


def shared_out(rng, own, number, rows, count, top, most, skew):
    order = jax.random.permutation(rng, count)
    heavy_load, common = shares(count, rows * top, most, skew, True), shares(count, rows * top, most, skew, False)
    places = jnp.arange(count)

    def named(lengths, rotation):
        used = int((lengths > 0).sum())
        fixed = max(1, used // 4)
        shifted = fixed + (places - fixed + rotation * (used - fixed)) % max(1, count - fixed)
        return jnp.zeros((count,), jnp.int32).at[order[jnp.where(places < fixed, places, shifted)]].set(jnp.asarray(lengths, jnp.int32))

    lengths = jnp.where(number % 4 == 0, named(heavy_load, number // 4), named(common, number - number // 4 - 1))
    mixed = jax.random.permutation(jax.random.fold_in(own, 3), count)
    source_of, sink = mixed[0:count // 2 * 2:2], mixed[1:count // 2 * 2:2]
    margin = jnp.minimum(lengths[source_of] - 1, most - lengths[sink]) // 2
    margin = jnp.where((source_of == order[0]) | (sink == order[0]) | (lengths[sink] == 0), 0, jnp.maximum(margin, 0))
    shifted = jax.random.randint(jax.random.fold_in(own, 4), (count // 2,), 0, 1 << 20) % (margin + 1)
    lengths = lengths.at[source_of].add(-shifted).at[sink].add(shifted)
    labels = jnp.searchsorted(jnp.cumsum(lengths), jnp.arange(rows * top), side="right").astype(jnp.int32)
    grid = labels.reshape(top, rows).T
    grid = grid[jax.random.permutation(jax.random.fold_in(own, 1), rows)]
    rotation = jax.random.randint(jax.random.fold_in(own, 2), (rows, 1), 0, top)
    return jnp.take_along_axis(grid, (jnp.arange(top)[None, :] + rotation) % top, axis=1)


def shares(count, total, most, lean, full):
    loads = [(1 << 20) // math.isqrt(rank ** lean) + 1 for rank in range(1, count + 1)]
    largest = most if full else min(most, max(-(-total // count), total * loads[0] // sum(loads)))
    least = 1 if total - largest >= count - 1 else 0
    given, spare = [largest] + [least] * (count - 1), total - largest - least * (count - 1)
    while spare > 0:
        free = [i for i in range(1, count) if given[i] < largest] or [i for i in range(1, count) if given[i] < most]
        mass, left = sum([loads[i] for i in free]), spare
        for i in free:
            more = min(most - given[i], max(1, left * loads[i] // mass), spare)
            given[i] = given[i] + more
            spare = spare - more
    return np.array(given)


def noise(own_key, extent, width, reach, shards=(), kind=jnp.bfloat16):
    array = jax.random.normal(own_key, extent, jnp.float32) * width
    if len(shards) > 0:
        array = block_levels(own_key, extent, shards, -0.22, 0.18) * array
    return jnp.clip(array, min=-reach, max=reach).astype(kind)


def setup_inputs(seed: int = 0) -> dict:
    seeds = jax.random.split(jax.random.key(seed), 7)
    a_vals = noise(seeds[0], (NBR, KA, BS, BS), 1.0, 6.0, ((0, 16), (1, 4)), jnp.float32)
    a_group_keys = jax.random.split(jax.random.fold_in(seeds[1], 1), NBR * KA // (RB * KA))
    a_group_turns = jax.random.permutation(jax.random.fold_in(seeds[1], 3), NBR * KA // (RB * KA))
    a_group = jax.vmap(lambda own, number: shared_out(jax.random.fold_in(seeds[1], 2), own, number, RB * KA, GROUPS, 1, CAP, 2))(a_group_keys, a_group_turns).reshape((NBR, KA, 1))
    a_offset = touch_ends(jax.random.randint(seeds[2], (NBR, KA), 0, KPG), jax.random.fold_in(seeds[2], 1), 0, KPG - 1).astype(jnp.int32)
    b_vals = noise(seeds[3], (NKB, N_ROW, KBG, BS, BS), BS ** -0.5, 0.5, ((0, 64), (1, 4)), jnp.float32)
    b_cols = touch_ends(jax.random.randint(seeds[4], (NKB, N_ROW, KBG), 0, JG), jax.random.fold_in(seeds[4], 1), 0, JG - 1).astype(jnp.int32)
    c_cols = draw_c_cols(jax.random.fold_in(seeds[6], 71), 0)
    return dict(a_vals=a_vals, a_group=a_group, a_offset=a_offset, b_vals=b_vals, b_cols=b_cols, c_cols=c_cols)


def reference(a_vals, a_group, a_offset, b_vals, b_cols, c_cols):
    a_cols = (a_group[:, :, 0] * KPG + a_offset).astype(jnp.int32)

    def one_row(inputs):
        blocks, columns, wanted = inputs
        b_rows = b_vals[columns]
        b_index = b_cols[columns]
        products = jnp.einsum("sab,srtbc->srtac", blocks, b_rows, precision=lax.Precision.HIGHEST)
        hitting = (b_index[:, :, :, None] == wanted[None, :, None, :]).astype(jnp.float32)
        return jnp.einsum("srtq,srtac->rqac", hitting, products, precision=lax.Precision.HIGHEST)

    return lax.map(one_row, (a_vals, a_cols, c_cols))
```

```python
import functools
import jax
import jax.numpy as jnp
from jax import lax
from jax.experimental import pallas as pl
from jax.experimental.pallas import tpu as pltpu
from jax.sharding import PartitionSpec as P

NZ = 8
NX = 4
PIECES = ((0, 4), (4, 8), (8, 12), (12, 15))
PLUS_ORDER = (0, 1, 2, 3)
MINUS_ORDER = (2, 3, 0, 1)
ROWS = 6
SLOTS = 3
KEPT = 4
TERMS = 3


def kernel(
    meta_ref, a_ref, b_ref, out_ref,
    b0, b1, b2, b3, b4, b5, b6, b7,
    a_all, acc, prod, half, far_in, near_in,
    meta_a, meta_b, table_v, table_s,
    loc_sem, tab_sem,
    ma_send, ma_recv, mb_send, mb_recv,
    bp_send, bp_recv, bm_send, bm_recv,
    y_send, y_recv, x_send, x_recv, t_send, t_recv,
    c_send, c_recv, r_send, r_recv,
):
    bufs = (b0, b1, b2, b3, b4, b5, b6, b7)
    x = lax.axis_index("row")
    col = lax.axis_index("col")
    rep = lax.axis_index("rep")
    z, y_lo = col % NZ, col // NZ
    core, y_hi = rep % 2, rep // 2
    y = y_hi * 2 + y_lo

    def at(x_, y_, z_, core_):
        return (x_, (y_ % 2) * NZ + z_, (y_ // 2) * 2 + core_)

    def z_at(step):
        return at(x, y, (z + step) % NZ, core)

    def x_at(step):
        return at((x + step) % NX, y, z, core)

    def y_at(step):
        return at(x, (y + step) % 4, z, core)

    sibling = at(x, y, z, 1 - core)
    y_pair = y_hi * 2 + (1 - y_lo)

    def copy(src, dst, send, recv, device):
        return pltpu.make_async_remote_copy(
            src_ref=src, dst_ref=dst, send_sem=send, recv_sem=recv,
            device_id=device, device_id_type=pl.DeviceIdType.MESH,
        )

    pairs = [(fy, rx) for fy in range(2) for rx in range(NX) if (fy, rx) != (0, 0)]

    def pair_at(fy, rx):
        return at((x + rx) % NX, y_hi * 2 + (y_lo + fy) % 2, z, core)

    peers = [z_at(r) for r in range(1, NZ)] + [pair_at(*p) for p in pairs]
    other_y = at(x, (y + 3 - 2 * y_lo) % 4, z, core)
    peers += [other_y, sibling]
    barrier = pltpu.get_barrier_semaphore()
    for peer in peers:
        pl.semaphore_signal(barrier, inc=1, device_id=peer, device_id_type=pl.DeviceIdType.MESH)
    pl.semaphore_wait(barrier, len(peers))

    sent = []

    def go(c):
        c.start()
        sent.append(c)
        return c

    to_z = [go(copy(meta_ref, meta_b.at[r], mb_send.at[r], mb_recv.at[r], z_at(r))) for r in range(1, NZ)]
    to_pair = [
        go(copy(meta_ref, meta_a.at[fy * NX + rx], ma_send.at[fy * NX + rx], ma_recv.at[fy * NX + rx], pair_at(fy, rx)))
        for fy, rx in pairs
    ]

    def ring(sign):
        sems = (bp_send, bp_recv) if sign > 0 else (bm_send, bm_recv)
        order = PLUS_ORDER if sign > 0 else MINUS_ORDER

        def hop(k, n):
            lo, hi = PIECES[order[n]]
            src = b_ref if k == 0 else bufs[(-sign * k) % NZ]
            dst = bufs[(-sign * (k + 1)) % NZ]
            return copy(
                src.at[pl.ds(lo, hi - lo)], dst.at[pl.ds(lo, hi - lo)],
                sems[0].at[k * 4 + n], sems[1].at[k * 4 + n], z_at(sign),
            )

        return hop

    plus, minus = ring(1), ring(-1)
    hops = {}
    for n in range(4):
        hops[1, 0, n] = go(plus(0, n))
        hops[-1, 0, n] = go(minus(0, n))

    own_b = pltpu.make_async_copy(b_ref, b0, loc_sem.at[0])
    own_b.start()
    span = ROWS * SLOTS
    cut = span // 2
    own_a = pltpu.make_async_copy(a_ref, a_all.at[pl.ds(0, span)], loc_sem.at[1])
    cross_a = copy(a_ref, a_all.at[pl.ds(0, span)], y_send, y_recv, at(x, y_pair, z, core))

    @pl.when(core == 0)
    def _():
        own_a.start()

    @pl.when(core == 1)
    def _():
        cross_a.start()

    meta_b[0] = meta_ref[...]
    meta_a[0] = meta_ref[...]
    for c in to_z + to_pair:
        c.wait_recv()
    lane = lax.broadcasted_iota(jnp.int32, (8, 128), 1)
    line = lax.broadcasted_iota(jnp.int32, (8, 128), 0)
    b_cols = jnp.concatenate([meta_b[(NZ - d) % NZ, 1:2, :] for d in range(NZ)], axis=0)
    away = (lane // 32 - x + NX) % NX
    inside = lane % 32
    place = jnp.where(away == 0, 0, jnp.where(away == 3, 1, jnp.where(away == 1, 2, 3))) * span + inside
    owner = jnp.zeros((8, 128), jnp.int32)
    for m in range(1, ROWS):
        owner = owner + jnp.where(inside >= SLOTS * m, 1, 0)
    group = (y_lo * NZ + (line + z) % NZ) * 4 + rep

    def pick(where, value):
        return jnp.sum(jnp.where(where, value, 0), axis=1, keepdims=True)

    for s in range(2):
        flip = (core + s) % 2
        base = flip * NX
        codes = meta_a[base, 0:1, :]
        for rx in range(1, NX):
            codes = codes + meta_a[base + rx, 0:1, :]
        codes = jnp.broadcast_to(codes, (8, 128)) - 1
        wanted = jnp.broadcast_to(meta_a[base, 2:3, :], (8, 128))
        match = (codes >= 0) & (codes // 8 == group)
        first = jnp.min(jnp.where(match, lane, 1000), axis=1, keepdims=True)
        last = jnp.max(jnp.where(match, lane, -1), axis=1, keepdims=True)
        result = jnp.zeros((8, 128), jnp.int32)
        for k in range(2):
            chosen = match & (lane == first) if k == 0 else match & (lane == last) & (lane != first)
            exists = pick(chosen, 1)
            index = pick(chosen, place + s * NX * span)
            offset = pick(chosen, codes % 8)
            row = pick(chosen, owner)
            result = result + jnp.where(lane == k * 32, index, 0)
            result = result + jnp.where(lane == k * 32 + 1, offset * TERMS, 0)
            result = result + jnp.where(lane == k * 32 + 2, row, 0)
            kept = [pick(lane == row * KEPT + q, wanted) for q in range(KEPT)]
            for t in range(TERMS):
                target = pick(lane == offset * TERMS + t, b_cols)
                for q in range(KEPT):
                    hit = jnp.where((target == kept[q]) & (exists > 0), 1, 0)
                    result = result + jnp.where(lane == k * 32 + 8 + t * KEPT + q, hit, 0)
        table_v[s] = result
    to_scalar = pltpu.make_async_copy(table_v, table_s, tab_sem)
    to_scalar.start()
    to_scalar.wait()

    @pl.when(core == 0)
    def _():
        own_a.wait()

    @pl.when(core == 1)
    def _():
        cross_a.wait_recv()

    def a_part(slot, lo, hi):
        return a_all.at[pl.ds(slot * span + lo, hi - lo)]

    xs = [
        copy(a_part(0, 0, cut), a_part(1, 0, cut), x_send.at[0], x_recv.at[0], x_at(1)),
        copy(a_part(0, cut, span), a_part(2, cut, span), x_send.at[1], x_recv.at[1], x_at(NX - 1)),
        copy(a_part(0, cut, span), a_part(1, cut, span), x_send.at[2], x_recv.at[2], x_at(1)),
        copy(a_part(0, 0, cut), a_part(2, 0, cut), x_send.at[3], x_recv.at[3], x_at(NX - 1)),
        copy(a_part(1, 0, cut), a_part(3, 0, cut), x_send.at[4], x_recv.at[4], x_at(1)),
        copy(a_part(2, cut, span), a_part(3, cut, span), x_send.at[5], x_recv.at[5], x_at(NX - 1)),
    ]
    ts = [
        copy(a_part(k, 0, span), a_part(NX + k, 0, span), t_send.at[k], t_recv.at[k], sibling)
        for k in range(NX)
    ]
    for c in xs[:4]:
        go(c)
    go(ts[0])

    def forward(k, n, p_on=True, m_on=True):
        hops[1, k - 1, n].wait_recv()
        if p_on:
            hops[1, k, n] = go(plus(k, n))
        hops[-1, k - 1, n].wait_recv()
        if m_on:
            hops[-1, k, n] = go(minus(k, n))

    for n in range(4):
        forward(1, n)
    xs[0].wait_recv()
    go(xs[4])
    xs[1].wait_recv()
    go(xs[5])
    xs[2].wait_recv()
    go(ts[1])
    xs[3].wait_recv()
    go(ts[2])
    for n in range(4):
        forward(2, n)
    xs[4].wait_recv()
    xs[5].wait_recv()
    go(ts[3])
    for c in ts:
        c.wait_recv()
    own_b.wait()

    def multiply(d, fresh):
        buf = bufs[d]

        def stream(s, carry):
            base = ((y_lo + core + s) % 2) * KEPT * ROWS
            for k in range(2):
                a = a_all[table_s[s, d, k * 32]]
                offset = table_s[s, d, k * 32 + 1]
                terms = [buf[offset + t] for t in range(TERMS)]
                chosen = []
                for q in range(KEPT):
                    weights = [table_s[s, d, k * 32 + 8 + t * KEPT + q].astype(jnp.float32) for t in range(TERMS)]
                    chosen.append(weights[0] * terms[0] + weights[1] * terms[1] + weights[2] * terms[2])
                b = jnp.concatenate(chosen, axis=1)
                a_hi = a.astype(jnp.bfloat16)
                a_lo = (a - a_hi.astype(jnp.float32)).astype(jnp.bfloat16)
                b_hi = b.astype(jnp.bfloat16)
                b_lo = (b - b_hi.astype(jnp.float32)).astype(jnp.bfloat16)
                dot = functools.partial(jnp.dot, preferred_element_type=jnp.float32)
                prod[k] = dot(a_hi, b_hi) + (dot(a_hi, b_lo) + dot(a_lo, b_hi))
            rows = [table_s[s, d, k * 32 + 2] for k in range(2)]

            def update(i, carry):
                w0 = jnp.where(rows[0] == i, 1.0, 0.0).astype(jnp.float32)
                w1 = jnp.where(rows[1] == i, 1.0, 0.0).astype(jnp.float32)
                for q in range(KEPT):
                    cols = pl.ds(q * 128, 128)
                    term = w0 * prod[0, :, cols] + w1 * prod[1, :, cols]
                    where = base + q * ROWS + i
                    acc[where] = term if fresh else acc[where] + term
                return carry

            return lax.fori_loop(0, ROWS, update, carry)

        lax.fori_loop(0, 2, stream, 0)

    multiply(0, True)
    forward(3, 0)
    multiply(1, False)
    forward(3, 1)
    multiply(7, False)
    forward(3, 2, False, False)
    multiply(2, False)
    multiply(6, False)
    forward(3, 3, False, False)
    multiply(3, False)
    multiply(5, False)
    for n in range(2):
        hops[1, 3, n].wait_recv()
        hops[-1, 3, n].wait_recv()
    multiply(4, False)

    def mine(step, which):
        dest = (y + step) % 4
        q = (dest // 2) * 2 + which
        return ((dest % 2) * KEPT + q) * ROWS

    cores = {}
    for step in (2, 1, 3, 0):
        cores[step] = go(copy(
            acc.at[pl.ds(mine(step, 1 - core), ROWS)], half.at[pl.ds(step * ROWS, ROWS)],
            c_send.at[step], c_recv.at[step], sibling,
        ))
    mid = ROWS // 2

    def fold(step):
        cores[step].wait_recv()
        start = mine(step, core)
        for i in range(ROWS):
            half[step * ROWS + i] = half[step * ROWS + i] + acc[start + i]

    def part(step, lo, hi):
        return half.at[pl.ds(step * ROWS + lo, hi - lo)]

    fold(2)
    far = [
        go(copy(part(2, 0, mid), far_in.at[pl.ds(0, mid)], r_send.at[0], r_recv.at[0], y_at(1))),
        go(copy(part(2, mid, ROWS), far_in.at[pl.ds(mid, ROWS - mid)], r_send.at[1], r_recv.at[1], y_at(3))),
    ]
    fold(1)
    near = [go(copy(part(1, mid, ROWS), near_in.at[pl.ds(mid, ROWS - mid)], r_send.at[2], r_recv.at[2], y_at(1)))]
    fold(3)
    near.append(go(copy(part(3, 0, mid), near_in.at[pl.ds(ROWS, mid)], r_send.at[3], r_recv.at[3], y_at(3))))
    fold(0)
    far[0].wait_recv()
    for i in range(mid):
        half[ROWS + i] = half[ROWS + i] + far_in[i]
    near.append(go(copy(part(1, 0, mid), near_in.at[pl.ds(0, mid)], r_send.at[4], r_recv.at[4], y_at(1))))
    far[1].wait_recv()
    for i in range(mid, ROWS):
        half[3 * ROWS + i] = half[3 * ROWS + i] + far_in[i]
    near.append(go(copy(part(3, mid, ROWS), near_in.at[pl.ds(ROWS + mid, ROWS - mid)], r_send.at[5], r_recv.at[5], y_at(3))))
    for c in near:
        c.wait_recv()
    for i in range(ROWS):
        out_ref[i] = half[i] + near_in[i] + near_in[ROWS + i]

    for c in sent:
        c.wait_send()

    @pl.when(core == 1)
    def _():
        cross_a.wait_send()


def local(a_vals, a_group, a_offset, b_vals, b_cols, c_cols):
    x = lax.axis_index("row")
    codes = (a_group[:, :, 0] * 8 + a_offset + 1).reshape(-1)
    lanes = jnp.arange(128, dtype=jnp.int32)
    codes = jnp.where(lanes // 32 == x, jnp.tile(jnp.pad(codes, (0, 32 - codes.shape[0])), 4), 0)
    meta = jnp.stack([
        codes,
        jnp.pad(b_cols.reshape(-1), (0, 128 - b_cols.size)),
        jnp.pad(c_cols.reshape(-1), (0, 128 - c_cols.size)),
    ])
    meta = jnp.pad(meta, ((0, 5), (0, 0)))
    a = a_vals.reshape(-1, 128, 128)
    b = b_vals.reshape(-1, 128, 128)
    blocks = lambda n: pltpu.VMEM((n, 128, 128), jnp.float32)
    dma = lambda n: pltpu.SemaphoreType.DMA((n,))
    out = pl.pallas_call(
        kernel,
        out_shape=jax.ShapeDtypeStruct((ROWS, 128, 128), jnp.float32),
        in_specs=[
            pl.BlockSpec(memory_space=pltpu.VMEM),
            pl.BlockSpec(memory_space=pl.ANY),
            pl.BlockSpec(memory_space=pl.ANY),
        ],
        out_specs=pl.BlockSpec(memory_space=pltpu.VMEM),
        scratch_shapes=[blocks(15) for _ in range(NZ)] + [
            blocks(2 * NX * ROWS * SLOTS),
            blocks(2 * KEPT * ROWS),
            pltpu.VMEM((2, 128, KEPT * 128), jnp.float32),
            blocks(4 * ROWS),
            blocks(ROWS),
            blocks(2 * ROWS),
            pltpu.VMEM((8, 8, 128), jnp.int32),
            pltpu.VMEM((8, 8, 128), jnp.int32),
            pltpu.VMEM((2, 8, 128), jnp.int32),
            pltpu.SMEM((2, 8, 128), jnp.int32),
            dma(2), pltpu.SemaphoreType.DMA,
            dma(8), dma(8), dma(8), dma(8),
            dma(16), dma(16), dma(16), dma(16),
            pltpu.SemaphoreType.DMA, pltpu.SemaphoreType.DMA,
            dma(6), dma(6), dma(4), dma(4),
            dma(4), dma(4), dma(6), dma(6),
        ],
        compiler_params=pltpu.CompilerParams(
            collective_id=0, has_side_effects=True, vmem_limit_bytes=48 * 1024 * 1024
        ),
        cost_estimate=pl.CostEstimate(flops=2 * 10 ** 9, bytes_accessed=3 * 10 ** 6, transcendentals=0),
    )(meta, a, b)
    return out.reshape(ROWS, 1, 1, 128, 128)


def solution(mesh):
    placed = (
        P("col", "row", None, None),
        P("col", "row", None),
        P("col", "row"),
        P(("col", "rep"), "row", None, None, None),
        P(("col", "rep"), "row", None),
        P("col", "row", None),
    )
    return jax.shard_map(
        local,
        mesh=mesh,
        in_specs=placed,
        out_specs=P("col", "row", "rep", None, None),
        check_vma=False,
    )
```

```python
import functools
import jax
import jax.numpy as jnp
from jax import lax
from jax.experimental import pallas as pl
from jax.experimental.pallas import tpu as pltpu
from jax.sharding import PartitionSpec as P

NZ = 8
NX = 4
PIECES = ((0, 8), (8, 15))
ROWS = 6
SLOTS = 3
KEPT = 4
TERMS = 3
KPG = 5
BLOCKS = KPG * TERMS
SPAN = ROWS * SLOTS
CUT = SPAN // 2
MID = ROWS // 2


def kernel(
    group_ref, offset_ref, b_cols_ref, c_cols_ref, a_ref, b_ref, out_ref,
    *scratch,
):
    bufs = (scratch[:NZ], scratch[NZ:2 * NZ])
    (
        b_own, a_all, acc, prod, core_in, packed, far_in, near_in,
        meta, meta_a, meta_b, table_v, table_s,
        loc_sem, tab_sem,
        ma_send, ma_recv, mb_send, mb_recv,
        bp_send, bp_recv, bm_send, bm_recv,
        y_send, y_recv, x_send, x_recv, t_send, t_recv,
        c_send, c_recv, r_send, r_recv,
    ) = scratch[2 * NZ:]
    x = lax.axis_index("row")
    col = lax.axis_index("col")
    rep = lax.axis_index("rep")
    z, y_lo = col % NZ, col // NZ
    core, y_hi = rep % 2, rep // 2
    y = y_hi * 2 + y_lo

    def at(x_, y_, z_, core_):
        return (x_, (y_ % 2) * NZ + z_, (y_ // 2) * 2 + core_)

    def z_at(step):
        return at(x, y, (z + step) % NZ, core)

    def x_at(step):
        return at((x + step) % NX, y, z, core)

    def y_at(step):
        return at(x, (y + step) % 4, z, core)

    def pair_at(fy, rx):
        return at((x + rx) % NX, y_hi * 2 + (y_lo + fy) % 2, z, core)

    sibling = at(x, y, z, 1 - core)
    other_y = at(x, (y + 3 - 2 * y_lo) % 4, z, core)

    def copy(src, dst, send, recv, device):
        return pltpu.make_async_remote_copy(
            src_ref=src, dst_ref=dst, send_sem=send, recv_sem=recv,
            device_id=device, device_id_type=pl.DeviceIdType.MESH,
        )

    pairs = [(fy, rx) for fy in range(2) for rx in range(NX) if (fy, rx) != (0, 0)]
    peers = [z_at(r) for r in range(1, NZ)] + [pair_at(*p) for p in pairs] + [other_y, sibling]
    barrier = pltpu.get_barrier_semaphore()
    for peer in peers:
        pl.semaphore_signal(barrier, inc=1, device_id=peer, device_id_type=pl.DeviceIdType.MESH)

    own_b = pltpu.make_async_copy(b_ref, b_own, loc_sem.at[0])
    own_b.start()
    own_a = pltpu.make_async_copy(a_ref, a_all.at[pl.ds(0, SPAN)], loc_sem.at[1])

    @pl.when(core == 0)
    def _():
        own_a.start()

    lane = lax.broadcasted_iota(jnp.int32, (8, 128), 1)
    line = lax.broadcasted_iota(jnp.int32, (8, 128), 0)
    spot = line * 128 + lane
    mine = jnp.zeros((8, 128), jnp.int32)
    for i in range(ROWS):
        for s in range(SLOTS):
            code = group_ref[s, 0, i] * 8 + offset_ref[s, i] + 1
            mine = jnp.where(spot == x * 32 + i * SLOTS + s, code, mine)
        for q in range(KEPT):
            mine = jnp.where(spot == 256 + i * KEPT + q, c_cols_ref[q, i], mine)
    for o in range(KPG):
        for t in range(TERMS):
            mine = jnp.where(spot == 128 + o * TERMS + t, b_cols_ref[t, 0, o], mine)
    meta[...] = mine
    meta_b[0] = mine
    meta_a[0] = mine

    left = lax.broadcasted_iota(jnp.int32, (64, 128), 1) < 64

    def to_halves(block):
        top, bottom = block[:64], block[64:]
        return (
            jnp.where(left, top, pltpu.roll(bottom, 64, 1)),
            jnp.where(left, pltpu.roll(top, 64, 1), bottom),
        )

    own_b.wait()

    def pack(n, carry):
        bufs[0][0][n], bufs[1][0][n] = to_halves(b_own[n])
        return carry

    lax.fori_loop(0, BLOCKS, pack, 0)
    pl.semaphore_wait(barrier, len(peers))

    sent = []

    def go(c):
        c.start()
        sent.append(c)
        return c

    hops = {}

    def hop(h, sign, k, n):
        sems = (bp_send, bp_recv) if sign > 0 else (bm_send, bm_recv)
        lo, hi = PIECES[n if sign > 0 else 1 - n]
        index = h * 8 + k * 2 + n
        hops[h, sign, k, n] = go(copy(
            bufs[h][(-sign * k) % NZ].at[pl.ds(lo, hi - lo)],
            bufs[h][(-sign * (k + 1)) % NZ].at[pl.ds(lo, hi - lo)],
            sems[0].at[index], sems[1].at[index], z_at(sign),
        ))

    def begin(h):
        for n in range(2):
            hop(h, 1, 0, n)
            hop(h, -1, 0, n)

    def forward(h, k, n, on=True):
        for sign in (1, -1):
            hops[h, sign, k - 1, n].wait_recv()
            if on:
                hop(h, sign, k, n)

    begin(0)
    cross_a = [
        copy(a_ref.at[pl.ds(0, CUT)], a_all.at[pl.ds(0, CUT)], y_send.at[0], y_recv.at[0], pair_at(1, 0)),
        copy(a_ref.at[pl.ds(CUT, SPAN - CUT)], a_all.at[pl.ds(CUT, SPAN - CUT)], y_send.at[1], y_recv.at[1], other_y),
    ]

    def a_part(slot, lo, hi):
        return a_all.at[pl.ds(slot * SPAN + lo, hi - lo)]

    xs = [
        copy(a_part(0, 0, CUT), a_part(1, 0, CUT), x_send.at[0], x_recv.at[0], x_at(1)),
        copy(a_part(0, CUT, SPAN), a_part(2, CUT, SPAN), x_send.at[1], x_recv.at[1], x_at(NX - 1)),
        copy(a_part(0, CUT, SPAN), a_part(1, CUT, SPAN), x_send.at[2], x_recv.at[2], x_at(1)),
        copy(a_part(0, 0, CUT), a_part(2, 0, CUT), x_send.at[3], x_recv.at[3], x_at(NX - 1)),
        copy(a_part(1, 0, CUT), a_part(3, 0, CUT), x_send.at[4], x_recv.at[4], x_at(1)),
        copy(a_part(2, CUT, SPAN), a_part(3, CUT, SPAN), x_send.at[5], x_recv.at[5], x_at(NX - 1)),
    ]
    ts = [
        copy(a_part(k, 0, SPAN), a_part(NX + k, 0, SPAN), t_send.at[k], t_recv.at[k], sibling)
        for k in range(NX)
    ]

    @pl.when(core == 1)
    def _():
        for c in cross_a:
            c.start()

    @pl.when(core == 0)
    def _():
        own_a.wait()
        for c in xs[:4]:
            c.start()

    to_z = [go(copy(meta, meta_b.at[r], mb_send.at[r], mb_recv.at[r], z_at(r))) for r in range(1, NZ)]
    to_pair = [
        go(copy(meta, meta_a.at[fy * NX + rx], ma_send.at[fy * NX + rx], ma_recv.at[fy * NX + rx], pair_at(fy, rx)))
        for fy, rx in pairs
    ]

    forward(0, 1, 0)

    @pl.when(core == 1)
    def _():
        for c in cross_a:
            c.wait_recv()
        for c in xs[:4]:
            c.start()

    sent.extend(xs[:4])
    go(ts[0])
    forward(0, 1, 1)

    for c in to_z + to_pair:
        c.wait_recv()
    b_cols = jnp.concatenate([meta_b[(NZ - d) % NZ, 1:2, :] for d in range(NZ)], axis=0)
    away = (lane // 32 - x + NX) % NX
    inside = lane % 32
    place = jnp.where(away == 0, 0, jnp.where(away == 3, 1, jnp.where(away == 1, 2, 3))) * SPAN + inside
    owner = jnp.zeros((8, 128), jnp.int32)
    for m in range(1, ROWS):
        owner = owner + jnp.where(inside >= SLOTS * m, 1, 0)
    group = (y_lo * NZ + (line + z) % NZ) * 4 + rep

    def pick(where, value):
        return jnp.sum(jnp.where(where, value, 0), axis=1, keepdims=True)

    for s in range(2):
        flip = (core + s) % 2
        base = flip * NX
        codes = meta_a[base, 0:1, :]
        for rx in range(1, NX):
            codes = codes + meta_a[base + rx, 0:1, :]
        codes = jnp.broadcast_to(codes, (8, 128)) - 1
        wanted = jnp.broadcast_to(meta_a[base, 2:3, :], (8, 128))
        match = (codes >= 0) & (codes // 8 == group)
        first = jnp.min(jnp.where(match, lane, 1000), axis=1, keepdims=True)
        last = jnp.max(jnp.where(match, lane, -1), axis=1, keepdims=True)
        result = jnp.zeros((8, 128), jnp.int32)
        for k in range(2):
            chosen = match & (lane == first) if k == 0 else match & (lane == last) & (lane != first)
            exists = pick(chosen, 1)
            index = pick(chosen, place + s * NX * SPAN)
            offset = pick(chosen, codes % 8)
            row = pick(chosen, owner)
            result = result + jnp.where(lane == k * 32, index, 0)
            result = result + jnp.where(lane == k * 32 + 1, offset * TERMS, 0)
            result = result + jnp.where(lane == k * 32 + 2, row, 0)
            kept = [pick(lane == row * KEPT + q, wanted) for q in range(KEPT)]
            for t in range(TERMS):
                target = pick(lane == offset * TERMS + t, b_cols)
                for q in range(KEPT):
                    hit = jnp.where((target == kept[q]) & (exists > 0), 1, 0)
                    result = result + jnp.where(lane == k * 32 + 8 + t * KEPT + q, hit, 0)
        table_v[s] = result
    to_scalar = pltpu.make_async_copy(table_v, table_s, tab_sem)
    to_scalar.start()
    to_scalar.wait()

    forward(0, 2, 0)
    forward(0, 2, 1)
    xs[0].wait_recv()
    go(xs[4])
    xs[1].wait_recv()
    go(xs[5])
    forward(0, 3, 0)
    begin(1)
    forward(0, 3, 1, False)
    xs[2].wait_recv()
    go(ts[1])
    xs[3].wait_recv()
    go(ts[2])

    def multiply(h, d, stream):
        buf = bufs[h][d]
        base = (h * 2 + (y_lo + core + stream) % 2) * 2 * ROWS
        for k in range(2):
            a = a_all[table_s[stream, d, k * 32]]
            offset = table_s[stream, d, k * 32 + 1]
            terms = [buf[offset + t] for t in range(TERMS)]
            chosen = []
            for q in range(KEPT):
                weights = [table_s[stream, d, k * 32 + 8 + t * KEPT + q].astype(jnp.float32) for t in range(TERMS)]
                chosen.append(weights[0] * terms[0] + weights[1] * terms[1] + weights[2] * terms[2])
            turned = [pltpu.roll(c, 64, 1) for c in chosen]
            b = jnp.concatenate([
                jnp.concatenate([jnp.where(left, chosen[g], turned[g + 2]) for g in range(2)], axis=1),
                jnp.concatenate([jnp.where(left, turned[g], chosen[g + 2]) for g in range(2)], axis=1),
            ], axis=0)
            a_hi = a.astype(jnp.bfloat16)
            a_lo = (a - a_hi.astype(jnp.float32)).astype(jnp.bfloat16)
            b_hi = b.astype(jnp.bfloat16)
            b_lo = (b - b_hi.astype(jnp.float32)).astype(jnp.bfloat16)
            dot = functools.partial(jnp.dot, preferred_element_type=jnp.float32)
            prod[k] = dot(a_hi, b_hi) + (dot(a_hi, b_lo) + dot(a_lo, b_hi))
        rows = [table_s[stream, d, k * 32 + 2] for k in range(2)]

        def update(i, carry):
            w0 = jnp.where(rows[0] == i, 1.0, 0.0).astype(jnp.float32)
            w1 = jnp.where(rows[1] == i, 1.0, 0.0).astype(jnp.float32)
            for g in range(2):
                cols = pl.ds(g * 128, 128)
                term = w0 * prod[0, :, cols] + w1 * prod[1, :, cols]
                where = base + g * ROWS + i
                acc[where] = term if d == 0 else acc[where] + term
            return carry

        lax.fori_loop(0, ROWS, update, 0)

    def multiply_all(h, *ds):
        for d in ds:
            def both(stream, carry, d=d):
                multiply(h, d, stream)
                return carry

            lax.fori_loop(0, 2, both, 0)

    cores, far, near = {}, {}, {}

    def to_sibling(h, e):
        start = (h * 4 + ((y_lo + e) % 2) * 2 + 1 - core) * ROWS
        cores[h, e] = go(copy(
            acc.at[pl.ds(start, ROWS)], core_in.at[pl.ds((h * 2 + e) * ROWS, ROWS)],
            c_send.at[h * 2 + e], c_recv.at[h * 2 + e], sibling,
        ))

    def fold(h, e):
        cores[h, e].wait_recv()
        lo = (y_lo + e) % 2
        start = (h * 4 + lo * 2 + core) * ROWS
        for i in range(ROWS):
            halves = to_halves(core_in[(h * 2 + e) * ROWS + i] + acc[start + i])
            packed[(h * 4 + lo) * ROWS + i] = halves[0]
            packed[(h * 4 + 2 + lo) * ROWS + i] = halves[1]

    def place_of(h, step):
        return (h * 4 + (y + step) % 4) * ROWS

    def send_y(h, step, lo, dst, dst_lo, index, way):
        return go(copy(
            packed.at[pl.ds(place_of(h, step) + lo, MID)], dst.at[pl.ds(dst_lo, MID)],
            r_send.at[h * 6 + index], r_recv.at[h * 6 + index], y_at(way),
        ))

    def fold_far(h):
        fold(h, 0)
        far[h] = [
            send_y(h, 2, 0, far_in, h * ROWS, 0, 1),
            send_y(h, 2, MID, far_in, h * ROWS + MID, 1, 3),
        ]

    def fold_near(h):
        fold(h, 1)
        near[h] = [
            send_y(h, 1, MID, near_in, h * 2 * ROWS + MID, 2, 1),
            send_y(h, 3, 0, near_in, h * 2 * ROWS + ROWS, 3, 3),
        ]

    def add_far(h):
        for way, lo in ((1, 0), (3, MID)):
            far[h][lo // MID].wait_recv()
            for i in range(lo, lo + MID):
                where = place_of(h, way) + i
                packed[where] = packed[where] + far_in[h * ROWS + i]
            near[h].append(send_y(
                h, way, lo, near_in, h * 2 * ROWS + (0 if way == 1 else ROWS) + lo, 4 + lo // MID, way,
            ))

    def finish(h):
        for c in near[h]:
            c.wait_recv()
        for i in range(ROWS):
            where = place_of(h, 0) + i
            base = h * 2 * ROWS + i
            packed[where] = packed[where] + near_in[base] + near_in[base + ROWS]

    forward(1, 1, 0)
    xs[4].wait_recv()
    xs[5].wait_recv()
    go(ts[3])
    for n in range(1):
        hops[0, 1, 3, n].wait_recv()
        hops[0, -1, 3, n].wait_recv()
    forward(1, 1, 1)
    for c in ts:
        c.wait_recv()
    multiply_all(0, 0, 1, 7)
    forward(1, 2, 0)
    multiply_all(0, 2, 6, 3, 5)
    forward(1, 2, 1)
    multiply_all(0, 4)
    to_sibling(0, 0)
    to_sibling(0, 1)
    multiply_all(1, 0)
    fold_far(0)
    fold_near(0)
    multiply_all(1, 1, 7)
    forward(1, 3, 0)
    multiply_all(1, 2, 6)
    add_far(0)
    forward(1, 3, 1, False)
    multiply_all(1, 3, 5)
    finish(0)
    hops[1, 1, 3, 0].wait_recv()
    hops[1, -1, 3, 0].wait_recv()
    multiply(1, 4, core)
    to_sibling(1, 0)
    multiply(1, 4, 1 - core)
    to_sibling(1, 1)
    fold_far(1)
    fold_near(1)
    add_far(1)
    finish(1)
    for i in range(ROWS):
        first, second = packed[place_of(0, 0) + i], packed[place_of(1, 0) + i]
        out_ref[i, pl.ds(0, 64)] = jnp.where(left, first, pltpu.roll(second, 64, 1))
        out_ref[i, pl.ds(64, 64)] = jnp.where(left, pltpu.roll(first, 64, 1), second)

    for c in sent:
        c.wait_send()

    @pl.when(core == 1)
    def _():
        for c in cross_a:
            c.wait_send()


def local(a_vals, a_group, a_offset, b_vals, b_cols, c_cols):
    a = a_vals.reshape(-1, 128, 128)
    b = b_vals.reshape(-1, 128, 128)
    blocks = lambda n: pltpu.VMEM((n, 128, 128), jnp.float32)
    thin = lambda n: pltpu.VMEM((n, 64, 128), jnp.float32)
    dma = lambda n: pltpu.SemaphoreType.DMA((n,))
    out = pl.pallas_call(
        kernel,
        out_shape=jax.ShapeDtypeStruct((ROWS, 128, 128), jnp.float32),
        in_specs=[pl.BlockSpec(memory_space=pltpu.SMEM)] * 4 + [pl.BlockSpec(memory_space=pltpu.HBM)] * 2,
        out_specs=pl.BlockSpec(memory_space=pltpu.VMEM),
        scratch_shapes=[thin(BLOCKS) for _ in range(2 * NZ)] + [
            blocks(BLOCKS),
            blocks(2 * NX * SPAN),
            blocks(2 * 4 * ROWS),
            pltpu.VMEM((2, 128, 256), jnp.float32),
            blocks(4 * ROWS),
            thin(2 * 4 * ROWS),
            thin(2 * ROWS),
            thin(4 * ROWS),
            pltpu.VMEM((8, 128), jnp.int32),
            pltpu.VMEM((8, 8, 128), jnp.int32),
            pltpu.VMEM((8, 8, 128), jnp.int32),
            pltpu.VMEM((2, 8, 128), jnp.int32),
            pltpu.SMEM((2, 8, 128), jnp.int32),
            dma(2), pltpu.SemaphoreType.DMA,
            dma(8), dma(8), dma(8), dma(8),
            dma(16), dma(16), dma(16), dma(16),
            dma(2), dma(2), dma(6), dma(6), dma(4), dma(4),
            dma(4), dma(4), dma(12), dma(12),
        ],
        compiler_params=pltpu.CompilerParams(
            collective_id=0, has_side_effects=True, vmem_limit_bytes=62 * 1024 * 1024
        ),
        cost_estimate=pl.CostEstimate(flops=2 * 10 ** 9, bytes_accessed=3 * 10 ** 6, transcendentals=0),
    )(
        a_group.transpose(1, 2, 0), a_offset.T, b_cols.transpose(2, 1, 0), c_cols[:, 0].T, a, b,
    )
    return out.reshape(ROWS, 1, 1, 128, 128)


def solution(mesh):
    placed = (
        P("col", "row", None, None),
        P("col", "row", None),
        P("col", "row"),
        P(("col", "rep"), "row", None, None, None),
        P(("col", "rep"), "row", None),
        P("col", "row", None),
    )
    return jax.shard_map(
        local,
        mesh=mesh,
        in_specs=placed,
        out_specs=P("col", "row", "rep", None, None),
        check_vma=False,
    )
```

```python
import functools
import jax
import jax.numpy as jnp
from jax import lax
from jax.experimental import pallas as pl
from jax.experimental.pallas import tpu as pltpu
from jax.sharding import PartitionSpec as P

NZ = 8
NX = 4
HALF_CUT = 8
QUARTER_CUT = 7
ROWS = 6
SLOTS = 3
KEPT = 4
TERMS = 3
KPG = 5
BLOCKS = KPG * TERMS
SPAN = ROWS * SLOTS
CUT = SPAN // 2
MID = ROWS // 2


def kernel(
    group_ref, offset_ref, b_cols_ref, c_cols_ref, a_ref, b_ref, out_ref,
    *scratch,
):
    bufs = (scratch[:NZ], scratch[NZ:2 * NZ], scratch[2 * NZ:3 * NZ])
    (
        b_own, a_all, prod, quarter_acc, own_core, core_in_0, core_in_1, core_in_2, acc,
        packed_0, packed_1, packed_2, far_0, far_1, far_2, near_0, near_1, near_2,
        meta, meta_a, meta_b, table_v, table_s,
        loc_sem, tab_sem,
        ma_send, ma_recv, mb_send, mb_recv,
        bp_send, bp_recv, bm_send, bm_recv,
        y_send, y_recv, x_send, x_recv, t_send, t_recv,
        c_send, c_recv, r_send, r_recv,
    ) = scratch[3 * NZ:]
    core_in = (core_in_0, core_in_1, core_in_2)
    packed = (packed_0, packed_1, packed_2)
    far_in = (far_0, far_1, far_2)
    near_in = (near_0, near_1, near_2)
    x = lax.axis_index("row")
    col = lax.axis_index("col")
    rep = lax.axis_index("rep")
    z, y_lo = col % NZ, col // NZ
    core, y_hi = rep % 2, rep // 2
    y = y_hi * 2 + y_lo

    def at(x_, y_, z_, core_):
        return (x_, (y_ % 2) * NZ + z_, (y_ // 2) * 2 + core_)

    def z_at(step):
        return at(x, y, (z + step) % NZ, core)

    def x_at(step):
        return at((x + step) % NX, y, z, core)

    def y_at(step):
        return at(x, (y + step) % 4, z, core)

    def pair_at(fy, rx):
        return at((x + rx) % NX, y_hi * 2 + (y_lo + fy) % 2, z, core)

    sibling = at(x, y, z, 1 - core)
    other_y = at(x, (y + 3 - 2 * y_lo) % 4, z, core)

    def copy(src, dst, send, recv, device):
        return pltpu.make_async_remote_copy(
            src_ref=src, dst_ref=dst, send_sem=send, recv_sem=recv,
            device_id=device, device_id_type=pl.DeviceIdType.MESH,
        )

    pairs = [(fy, rx) for fy in range(2) for rx in range(NX) if (fy, rx) != (0, 0)]
    peers = [z_at(r) for r in range(1, NZ)] + [pair_at(*p) for p in pairs] + [other_y, sibling]
    barrier = pltpu.get_barrier_semaphore()
    for peer in peers:
        pl.semaphore_signal(barrier, inc=1, device_id=peer, device_id_type=pl.DeviceIdType.MESH)

    own_b = pltpu.make_async_copy(b_ref, b_own, loc_sem.at[0])
    own_b.start()
    own_a = pltpu.make_async_copy(a_ref, a_all.at[pl.ds(0, SPAN)], loc_sem.at[1])

    @pl.when(core == 0)
    def _():
        own_a.start()

    lane = lax.broadcasted_iota(jnp.int32, (8, 128), 1)
    line = lax.broadcasted_iota(jnp.int32, (8, 128), 0)
    spot = line * 128 + lane
    mine = jnp.zeros((8, 128), jnp.int32)
    for i in range(ROWS):
        for s in range(SLOTS):
            code = group_ref[s, 0, i] * 8 + offset_ref[s, i] + 1
            mine = jnp.where(spot == x * 32 + i * SLOTS + s, code, mine)
        for q in range(KEPT):
            mine = jnp.where(spot == 256 + i * KEPT + q, c_cols_ref[q, i], mine)
    for o in range(KPG):
        for t in range(TERMS):
            mine = jnp.where(spot == 128 + o * TERMS + t, b_cols_ref[t, 0, o], mine)
    meta[...] = mine
    meta_b[0] = mine
    meta_a[0] = mine

    left = lax.broadcasted_iota(jnp.int32, (64, 128), 1) < 64

    def to_halves(block):
        top, bottom = block[:64], block[64:]
        return (
            jnp.where(left, top, pltpu.roll(bottom, 64, 1)),
            jnp.where(left, pltpu.roll(top, 64, 1), bottom),
        )

    even = lax.broadcasted_iota(jnp.int32, (32, 128), 1) % 64 < 32
    left_thin = left[:32]

    def to_quarters(half):
        top, bottom = half[:32], half[32:]
        return (
            jnp.where(even, top, pltpu.roll(bottom, 32, 1)),
            jnp.where(even, pltpu.roll(top, 96, 1), bottom),
        )

    own_b.wait()

    def pack(n, carry):
        bufs[0][0][n], half = to_halves(b_own[n])
        bufs[1][0][n], bufs[2][0][n] = to_quarters(half)
        return carry

    lax.fori_loop(0, BLOCKS, pack, 0)
    pl.semaphore_wait(barrier, len(peers))

    sent = []

    def go(c):
        c.start()
        sent.append(c)
        return c

    hops = {}

    def hop(h, sign, k, n):
        sems = (bp_send, bp_recv) if sign > 0 else (bm_send, bm_recv)
        split = HALF_CUT if h == 0 else QUARTER_CUT
        lo, hi = (0, split) if (n == 0) == (sign > 0) else (split, BLOCKS)
        index = h * 8 + k * 2 + n
        hops[h, sign, k, n] = go(copy(
            bufs[h][(-sign * k) % NZ].at[pl.ds(lo, hi - lo)],
            bufs[h][(-sign * (k + 1)) % NZ].at[pl.ds(lo, hi - lo)],
            sems[0].at[index], sems[1].at[index], z_at(sign),
        ))

    def begin(h):
        for n in range(2):
            hop(h, 1, 0, n)
            hop(h, -1, 0, n)

    def forward(h, k, n, on=True):
        for sign in (1, -1):
            hops[h, sign, k - 1, n].wait_recv()
            if on:
                hop(h, sign, k, n)

    begin(0)
    begin(1)
    cross_a = [
        copy(a_ref.at[pl.ds(0, CUT)], a_all.at[pl.ds(0, CUT)], y_send.at[0], y_recv.at[0], pair_at(1, 0)),
        copy(a_ref.at[pl.ds(CUT, SPAN - CUT)], a_all.at[pl.ds(CUT, SPAN - CUT)], y_send.at[1], y_recv.at[1], other_y),
    ]

    def a_part(slot, lo, hi):
        return a_all.at[pl.ds(slot * SPAN + lo, hi - lo)]

    xs = [
        copy(a_part(0, 0, CUT), a_part(1, 0, CUT), x_send.at[0], x_recv.at[0], x_at(1)),
        copy(a_part(0, CUT, SPAN), a_part(2, CUT, SPAN), x_send.at[1], x_recv.at[1], x_at(NX - 1)),
        copy(a_part(0, CUT, SPAN), a_part(1, CUT, SPAN), x_send.at[2], x_recv.at[2], x_at(1)),
        copy(a_part(0, 0, CUT), a_part(2, 0, CUT), x_send.at[3], x_recv.at[3], x_at(NX - 1)),
        copy(a_part(1, 0, CUT), a_part(3, 0, CUT), x_send.at[4], x_recv.at[4], x_at(1)),
        copy(a_part(2, CUT, SPAN), a_part(3, CUT, SPAN), x_send.at[5], x_recv.at[5], x_at(NX - 1)),
    ]
    ts = [
        copy(a_part(k, 0, SPAN), a_part(NX + k, 0, SPAN), t_send.at[k], t_recv.at[k], sibling)
        for k in range(NX)
    ]

    @pl.when(core == 1)
    def _():
        for c in cross_a:
            c.start()

    @pl.when(core == 0)
    def _():
        own_a.wait()
        for c in xs[:4]:
            c.start()

    to_z = [go(copy(meta, meta_b.at[r], mb_send.at[r], mb_recv.at[r], z_at(r))) for r in range(1, NZ)]
    to_pair = [
        go(copy(meta, meta_a.at[fy * NX + rx], ma_send.at[fy * NX + rx], ma_recv.at[fy * NX + rx], pair_at(fy, rx)))
        for fy, rx in pairs
    ]

    forward(0, 1, 0)

    @pl.when(core == 1)
    def _():
        for c in cross_a:
            c.wait_recv()
        for c in xs[:4]:
            c.start()

    sent.extend(xs[:4])
    go(ts[0])
    forward(0, 1, 1)
    forward(1, 1, 0)
    forward(1, 1, 1)

    for c in to_z + to_pair:
        c.wait_recv()
    b_cols = jnp.concatenate([meta_b[(NZ - d) % NZ, 1:2, :] for d in range(NZ)], axis=0)
    away = (lane // 32 - x + NX) % NX
    inside = lane % 32
    place = jnp.where(away == 0, 0, jnp.where(away == 3, 1, jnp.where(away == 1, 2, 3))) * SPAN + inside
    owner = jnp.zeros((8, 128), jnp.int32)
    for m in range(1, ROWS):
        owner = owner + jnp.where(inside >= SLOTS * m, 1, 0)
    group = (y_lo * NZ + (line + z) % NZ) * 4 + rep

    def pick(where, value):
        return jnp.sum(jnp.where(where, value, 0), axis=1, keepdims=True)

    for s in range(2):
        flip = (core + s) % 2
        base = flip * NX
        codes = meta_a[base, 0:1, :]
        for rx in range(1, NX):
            codes = codes + meta_a[base + rx, 0:1, :]
        codes = jnp.broadcast_to(codes, (8, 128)) - 1
        wanted = jnp.broadcast_to(meta_a[base, 2:3, :], (8, 128))
        match = (codes >= 0) & (codes // 8 == group)
        first = jnp.min(jnp.where(match, lane, 1000), axis=1, keepdims=True)
        last = jnp.max(jnp.where(match, lane, -1), axis=1, keepdims=True)
        result = jnp.zeros((8, 128), jnp.int32)
        for k in range(2):
            chosen = match & (lane == first) if k == 0 else match & (lane == last) & (lane != first)
            exists = pick(chosen, 1)
            index = pick(chosen, place + s * NX * SPAN)
            offset = pick(chosen, codes % 8)
            row = pick(chosen, owner)
            result = result + jnp.where(lane == k * 32, index, 0)
            result = result + jnp.where(lane == k * 32 + 1, offset * TERMS, 0)
            result = result + jnp.where(lane == k * 32 + 2, row, 0)
            kept = [pick(lane == row * KEPT + q, wanted) for q in range(KEPT)]
            for t in range(TERMS):
                target = pick(lane == offset * TERMS + t, b_cols)
                for q in range(KEPT):
                    hit = jnp.where((target == kept[q]) & (exists > 0), 1, 0)
                    result = result + jnp.where(lane == k * 32 + 8 + t * KEPT + q, hit, 0)
        table_v[s] = result
    to_scalar = pltpu.make_async_copy(table_v, table_s, tab_sem)
    to_scalar.start()
    to_scalar.wait()

    forward(0, 2, 0)
    forward(0, 2, 1)
    forward(1, 2, 0)
    forward(1, 2, 1)
    xs[0].wait_recv()
    go(xs[4])
    xs[1].wait_recv()
    go(xs[5])
    forward(0, 3, 0)
    begin(2)
    forward(0, 3, 1, False)
    xs[2].wait_recv()
    go(ts[1])
    xs[3].wait_recv()
    go(ts[2])

    def multiply(h, ds, stream):
        lo = (y_lo + core + stream) % 2
        base = lo * 2 * ROWS if h == 0 else ((h - 1) * 2 + lo) * ROWS
        into = acc if h == 0 else quarter_acc
        slots = [(d, k) for d in ds for k in range(2)]
        for d, k in slots:
            buf = bufs[h][d]
            a = a_all[table_s[stream, d, k * 32]]
            offset = table_s[stream, d, k * 32 + 1]
            terms = [buf[offset + t] for t in range(TERMS)]
            chosen = []
            for q in range(KEPT):
                weights = [table_s[stream, d, k * 32 + 8 + t * KEPT + q].astype(jnp.float32) for t in range(TERMS)]
                chosen.append(weights[0] * terms[0] + weights[1] * terms[1] + weights[2] * terms[2])
            turned = [pltpu.roll(c, 64, 1) for c in chosen]
            if h == 0:
                b = jnp.concatenate([
                    jnp.concatenate([jnp.where(left, chosen[g], turned[g + 2]) for g in range(2)], axis=1),
                    jnp.concatenate([jnp.where(left, turned[g], chosen[g + 2]) for g in range(2)], axis=1),
                ], axis=0)
            else:
                parts = []
                for upper in (True, False):
                    pair = [
                        jnp.where(left_thin, chosen[g], turned[g + 1]) if upper
                        else jnp.where(left_thin, turned[g], chosen[g + 1])
                        for g in (0, 2)
                    ]
                    parts.append(jnp.where(even, pair[0], pltpu.roll(pair[1], 32, 1)))
                    parts.append(jnp.where(even, pltpu.roll(pair[0], 96, 1), pair[1]))
                b = jnp.concatenate(parts, axis=0)
            a_hi = a.astype(jnp.bfloat16)
            a_lo = (a - a_hi.astype(jnp.float32)).astype(jnp.bfloat16)
            b_hi = b.astype(jnp.bfloat16)
            b_lo = (b - b_hi.astype(jnp.float32)).astype(jnp.bfloat16)
            dot = functools.partial(jnp.dot, preferred_element_type=jnp.float32)
            prod[slots.index((d, k)), :, pl.ds(0, b.shape[1])] = dot(a_hi, b_hi) + (dot(a_hi, b_lo) + dot(a_lo, b_hi))
        rows = [table_s[stream, d, k * 32 + 2] for d, k in slots]

        def update(i, carry):
            weights = [jnp.where(row == i, 1.0, 0.0).astype(jnp.float32) for row in rows]
            for g in range(2 if h == 0 else 1):
                where = base + g * ROWS + i
                total = None if 0 in ds else into[where]
                for n, weight in enumerate(weights):
                    term = weight * prod[n, :, pl.ds(g * 128, 128)]
                    total = term if total is None else total + term
                into[where] = total
            return carry

        lax.fori_loop(0, ROWS, update, 0)

    def multiply_all(h, *ds):
        def both(stream, carry):
            multiply(h, ds, stream)
            return carry

        lax.fori_loop(0, 2, both, 0)

    cores, far, near = {}, {}, {}

    def to_sibling(h, e):
        lo = (y_lo + e) % 2
        if h == 0:
            src = acc.at[pl.ds((lo * 2 + 1 - core) * ROWS, ROWS)]
        else:
            for i in range(ROWS):
                halves = to_halves(quarter_acc[((h - 1) * 2 + lo) * ROWS + i])
                for c in range(2):
                    own_core[(((h - 1) * 2 + lo) * 2 + c) * ROWS + i] = halves[c]
            src = own_core.at[pl.ds((((h - 1) * 2 + lo) * 2 + 1 - core) * ROWS, ROWS)]
        cores[h, e] = go(copy(
            src, core_in[h].at[pl.ds(e * ROWS, ROWS)], c_send.at[h * 2 + e], c_recv.at[h * 2 + e], sibling,
        ))

    def fold(h, e):
        cores[h, e].wait_recv()
        lo = (y_lo + e) % 2
        for i in range(ROWS):
            if h == 0:
                pieces = to_halves(core_in[h][e * ROWS + i] + acc[(lo * 2 + core) * ROWS + i])
            else:
                pieces = to_quarters(
                    core_in[h][e * ROWS + i] + own_core[(((h - 1) * 2 + lo) * 2 + core) * ROWS + i]
                )
            packed[h][lo * ROWS + i] = pieces[0]
            packed[h][(2 + lo) * ROWS + i] = pieces[1]

    def place_of(h, step):
        return ((y + step) % 4) * ROWS

    def send_y(h, step, lo, dst, dst_lo, index, way):
        return go(copy(
            packed[h].at[pl.ds(place_of(h, step) + lo, MID)], dst.at[pl.ds(dst_lo, MID)],
            r_send.at[h * 6 + index], r_recv.at[h * 6 + index], y_at(way),
        ))

    def fold_far(h):
        fold(h, 0)
        far[h] = [
            send_y(h, 2, 0, far_in[h], 0, 0, 1),
            send_y(h, 2, MID, far_in[h], MID, 1, 3),
        ]

    def fold_near(h):
        fold(h, 1)
        near[h] = [
            send_y(h, 1, MID, near_in[h], MID, 2, 1),
            send_y(h, 3, 0, near_in[h], ROWS, 3, 3),
        ]

    def add_far(h):
        for way, lo in ((1, 0), (3, MID)):
            far[h][lo // MID].wait_recv()
            for i in range(lo, lo + MID):
                where = place_of(h, way) + i
                packed[h][where] = packed[h][where] + far_in[h][i]
            near[h].append(send_y(
                h, way, lo, near_in[h], (0 if way == 1 else ROWS) + lo, 4 + lo // MID, way,
            ))

    def finish(h):
        for c in near[h]:
            c.wait_recv()
        for i in range(ROWS):
            where = place_of(h, 0) + i
            packed[h][where] = packed[h][where] + near_in[h][i] + near_in[h][ROWS + i]

    def last(h):
        hops[h, 1, 3, 0].wait_recv()
        hops[h, -1, 3, 0].wait_recv()

    xs[4].wait_recv()
    xs[5].wait_recv()
    go(ts[3])
    forward(1, 3, 0)
    forward(1, 3, 1, False)
    for c in ts:
        c.wait_recv()
    multiply_all(0, 0, 1, 7)
    multiply_all(0, 2, 6)
    forward(2, 1, 0)
    multiply_all(1, 0, 1, 7)
    multiply_all(1, 2, 6)
    forward(2, 1, 1)
    last(0)
    multiply_all(0, 3, 5, 4)
    to_sibling(0, 0)
    to_sibling(0, 1)
    last(1)
    multiply_all(1, 3, 5, 4)
    to_sibling(1, 0)
    to_sibling(1, 1)
    forward(2, 2, 0)
    fold_far(0)
    fold_far(1)
    fold_near(0)
    fold_near(1)
    forward(2, 2, 1)
    multiply_all(2, 0, 1, 7)
    add_far(0)
    add_far(1)
    forward(2, 3, 0)
    multiply_all(2, 2, 6)
    forward(2, 3, 1, False)
    multiply_all(2, 3, 5)
    last(2)
    multiply(2, (4,), core)
    to_sibling(2, 0)
    multiply(2, (4,), 1 - core)
    to_sibling(2, 1)
    finish(0)
    finish(1)
    fold_far(2)
    fold_near(2)
    add_far(2)
    finish(2)
    for i in range(ROWS):
        where = place_of(0, 0) + i
        first, third, fourth = packed[0][where], packed[1][where], packed[2][where]
        second = jnp.concatenate([
            jnp.where(even, third, pltpu.roll(fourth, 32, 1)),
            jnp.where(even, pltpu.roll(third, 96, 1), fourth),
        ], axis=0)
        out_ref[i, pl.ds(0, 64)] = jnp.where(left, first, pltpu.roll(second, 64, 1))
        out_ref[i, pl.ds(64, 64)] = jnp.where(left, pltpu.roll(first, 64, 1), second)

    for c in sent:
        c.wait_send()

    @pl.when(core == 1)
    def _():
        for c in cross_a:
            c.wait_send()


def local(a_vals, a_group, a_offset, b_vals, b_cols, c_cols):
    a = a_vals.reshape(-1, 128, 128)
    b = b_vals.reshape(-1, 128, 128)
    blocks = lambda n: pltpu.VMEM((n, 128, 128), jnp.float32)
    thin = lambda n: pltpu.VMEM((n, 64, 128), jnp.float32)
    slim = lambda n: pltpu.VMEM((n, 32, 128), jnp.float32)
    dma = lambda n: pltpu.SemaphoreType.DMA((n,))
    out = pl.pallas_call(
        kernel,
        out_shape=jax.ShapeDtypeStruct((ROWS, 128, 128), jnp.float32),
        in_specs=[pl.BlockSpec(memory_space=pltpu.SMEM)] * 4 + [pl.BlockSpec(memory_space=pltpu.HBM)] * 2,
        out_specs=pl.BlockSpec(memory_space=pltpu.VMEM),
        scratch_shapes=[thin(BLOCKS)] * NZ + [slim(BLOCKS)] * (2 * NZ) + [
            blocks(BLOCKS),
            blocks(2 * NX * SPAN),
            pltpu.VMEM((8, 128, 256), jnp.float32),
            blocks(4 * ROWS), thin(8 * ROWS),
            blocks(2 * ROWS), thin(2 * ROWS), thin(2 * ROWS),
            blocks(4 * ROWS),
            thin(4 * ROWS), slim(4 * ROWS), slim(4 * ROWS),
            thin(ROWS), slim(ROWS), slim(ROWS),
            thin(2 * ROWS), slim(2 * ROWS), slim(2 * ROWS),
            pltpu.VMEM((8, 128), jnp.int32),
            pltpu.VMEM((8, 8, 128), jnp.int32),
            pltpu.VMEM((8, 8, 128), jnp.int32),
            pltpu.VMEM((2, 8, 128), jnp.int32),
            pltpu.SMEM((2, 8, 128), jnp.int32),
            dma(2), pltpu.SemaphoreType.DMA,
            dma(8), dma(8), dma(8), dma(8),
            dma(24), dma(24), dma(24), dma(24),
            dma(2), dma(2), dma(6), dma(6), dma(4), dma(4),
            dma(6), dma(6), dma(18), dma(18),
        ],
        compiler_params=pltpu.CompilerParams(
            collective_id=0, has_side_effects=True, vmem_limit_bytes=62 * 1024 * 1024
        ),
        cost_estimate=pl.CostEstimate(flops=2 * 10 ** 9, bytes_accessed=3 * 10 ** 6, transcendentals=0),
    )(
        a_group.transpose(1, 2, 0), a_offset.T, b_cols.transpose(2, 1, 0), c_cols[:, 0].T, a, b,
    )
    return out.reshape(ROWS, 1, 1, 128, 128)


def solution(mesh):
    placed = (
        P("col", "row", None, None),
        P("col", "row", None),
        P("col", "row"),
        P(("col", "rep"), "row", None, None, None),
        P(("col", "rep"), "row", None),
        P("col", "row", None),
    )
    return jax.shard_map(
        local,
        mesh=mesh,
        in_specs=placed,
        out_specs=P("col", "row", "rep", None, None),
        check_vma=False,
    )
```

```python
import functools
import jax
import jax.numpy as jnp
from jax import lax
from jax.experimental import pallas as pl
from jax.experimental.pallas import tpu as pltpu
from jax.sharding import PartitionSpec as P

NZ = 8
NX = 4
HALF_CUT = 8
QUARTER_CUT = 7
ROWS = 6
SLOTS = 3
KEPT = 4
TERMS = 3
KPG = 5
BLOCKS = KPG * TERMS
SPAN = ROWS * SLOTS
CUT = SPAN // 2
MID = ROWS // 2


def kernel(
    group_ref, offset_ref, b_cols_ref, c_cols_ref, a_ref, b_ref, out_ref,
    *scratch,
):
    bufs = (scratch[:NZ], scratch[NZ:2 * NZ], scratch[2 * NZ:3 * NZ])
    (
        b_own, a_all, prod, quarter_acc, own_core, core_in_0, core_in_1, core_in_2, acc,
        packed_0, packed_1, packed_2, far_0, far_1, far_2, near_0, near_1, near_2,
        meta_a, meta_b, table_v, table_s,
        loc_sem, tab_sem,
        ma_send, ma_recv, mb_send, mb_recv,
        bp_send, bp_recv, bm_send, bm_recv,
        y_send, y_recv, x_send, x_recv, t_send, t_recv,
        c_send, c_recv, r_send, r_recv,
    ) = scratch[3 * NZ:]
    core_in = (core_in_0, core_in_1, core_in_2)
    packed = (packed_0, packed_1, packed_2)
    far_in = (far_0, far_1, far_2)
    near_in = (near_0, near_1, near_2)
    x = lax.axis_index("row")
    col = lax.axis_index("col")
    rep = lax.axis_index("rep")
    z, y_lo = col % NZ, col // NZ
    core, y_hi = rep % 2, rep // 2
    y = y_hi * 2 + y_lo

    def at(x_, y_, z_, core_):
        return (x_, (y_ % 2) * NZ + z_, (y_ // 2) * 2 + core_)

    def z_at(step):
        return at(x, y, (z + step) % NZ, core)

    def x_at(step):
        return at((x + step) % NX, y, z, core)

    def y_at(step):
        return at(x, (y + step) % 4, z, core)

    def pair_at(fy, rx):
        return at((x + rx) % NX, y_hi * 2 + (y_lo + fy) % 2, z, core)

    sibling = at(x, y, z, 1 - core)
    other_y = at(x, (y + 3 - 2 * y_lo) % 4, z, core)

    def copy(src, dst, send, recv, device):
        return pltpu.make_async_remote_copy(
            src_ref=src, dst_ref=dst, send_sem=send, recv_sem=recv,
            device_id=device, device_id_type=pl.DeviceIdType.MESH,
        )

    peers = [z_at(r) for r in (1, 2, NZ - 2, NZ - 1)] + [x_at(r) for r in range(1, NX)]
    peers += [pair_at(1, 0), other_y, sibling]
    barrier = pltpu.get_barrier_semaphore()
    for peer in peers:
        pl.semaphore_signal(barrier, inc=1, device_id=peer, device_id_type=pl.DeviceIdType.MESH)

    own_b = pltpu.make_async_copy(b_ref, b_own, loc_sem.at[0])
    own_b.start()
    own_a = pltpu.make_async_copy(a_ref, a_all.at[pl.ds(0, SPAN)], loc_sem.at[1])

    @pl.when(core == 0)
    def _():
        own_a.start()

    lane = lax.broadcasted_iota(jnp.int32, (8, 128), 1)
    line = lax.broadcasted_iota(jnp.int32, (8, 128), 0)
    spot = line * 128 + lane
    mine = jnp.zeros((8, 128), jnp.int32)
    for i in range(ROWS):
        for s in range(SLOTS):
            code = group_ref[s, 0, i] * 8 + offset_ref[s, i] + 1
            mine = jnp.where(spot == x * 32 + i * SLOTS + s, code, mine)
        for q in range(KEPT):
            mine = jnp.where(spot == 256 + i * KEPT + q, c_cols_ref[q, i], mine)
    for o in range(KPG):
        for t in range(TERMS):
            mine = jnp.where(spot == 128 + o * TERMS + t, b_cols_ref[t, 0, o], mine)
    meta_b[0] = mine
    meta_a[0] = mine

    left = lax.broadcasted_iota(jnp.int32, (64, 128), 1) < 64

    def to_halves(block):
        top, bottom = block[:64], block[64:]
        return (
            jnp.where(left, top, pltpu.roll(bottom, 64, 1)),
            jnp.where(left, pltpu.roll(top, 64, 1), bottom),
        )

    even = lax.broadcasted_iota(jnp.int32, (32, 128), 1) % 64 < 32
    left_thin = left[:32]

    def to_quarters(half):
        top, bottom = half[:32], half[32:]
        return (
            jnp.where(even, top, pltpu.roll(bottom, 32, 1)),
            jnp.where(even, pltpu.roll(top, 96, 1), bottom),
        )

    own_b.wait()

    def pack(n, carry):
        bufs[0][0][n], half = to_halves(b_own[n])
        bufs[1][0][n], bufs[2][0][n] = to_quarters(half)
        return carry

    lax.fori_loop(0, BLOCKS, pack, 0)
    pl.semaphore_wait(barrier, len(peers))

    sent = []

    def go(c):
        c.start()
        sent.append(c)
        return c

    hops = {}

    def hop(h, sign, k, n):
        sems = (bp_send, bp_recv) if sign > 0 else (bm_send, bm_recv)
        split = HALF_CUT if h == 0 else QUARTER_CUT
        lo, hi = (0, split) if (n == 0) == (sign > 0) else (split, BLOCKS)
        if h == 1 and k < 3:
            lo, hi = 0, BLOCKS
        index = h * 8 + k * 2 + n
        hops[h, sign, k, n] = go(copy(
            bufs[h][(-sign * k) % NZ].at[pl.ds(lo, hi - lo)],
            bufs[h][(-sign * (k + 1)) % NZ].at[pl.ds(lo, hi - lo)],
            sems[0].at[index], sems[1].at[index], z_at(sign),
        ))

    def begin(h):
        for n in range(1 if h == 1 else 2):
            hop(h, 1, 0, n)
            hop(h, -1, 0, n)

    def forward(h, k, n, on=True):
        for sign in (1, -1):
            hops[h, sign, k - 1, n].wait_recv()
            if on:
                hop(h, sign, k, n)

    begin(0)
    begin(1)
    cross_a = [
        copy(a_ref.at[pl.ds(0, CUT)], a_all.at[pl.ds(0, CUT)], y_send.at[0], y_recv.at[0], pair_at(1, 0)),
        copy(a_ref.at[pl.ds(CUT, SPAN - CUT)], a_all.at[pl.ds(CUT, SPAN - CUT)], y_send.at[1], y_recv.at[1], other_y),
    ]

    def a_part(slot, lo, hi):
        return a_all.at[pl.ds(slot * SPAN + lo, hi - lo)]

    xs = [
        copy(a_part(0, 0, CUT), a_part(1, 0, CUT), x_send.at[0], x_recv.at[0], x_at(1)),
        copy(a_part(0, CUT, SPAN), a_part(2, CUT, SPAN), x_send.at[1], x_recv.at[1], x_at(NX - 1)),
        copy(a_part(0, CUT, SPAN), a_part(1, CUT, SPAN), x_send.at[2], x_recv.at[2], x_at(1)),
        copy(a_part(0, 0, CUT), a_part(2, 0, CUT), x_send.at[3], x_recv.at[3], x_at(NX - 1)),
        copy(a_part(1, 0, CUT), a_part(3, 0, CUT), x_send.at[4], x_recv.at[4], x_at(1)),
        copy(a_part(2, CUT, SPAN), a_part(3, CUT, SPAN), x_send.at[5], x_recv.at[5], x_at(NX - 1)),
    ]
    ts = [
        copy(a_part(k, 0, SPAN), a_part(NX + k, 0, SPAN), t_send.at[k], t_recv.at[k], sibling)
        for k in range(NX)
    ]

    @pl.when(core == 1)
    def _():
        for c in cross_a:
            c.start()

    @pl.when(core == 0)
    def _():
        own_a.wait()
        for c in xs[:4]:
            c.start()

    on_z, on_a = {}, {}

    def index_z(src, dst, step):
        on_z[dst] = go(copy(meta_b.at[src], meta_b.at[dst], mb_send.at[dst], mb_recv.at[dst], z_at(step)))

    def index_a(src, dst, device):
        on_a[dst] = go(copy(meta_a.at[src], meta_a.at[dst], ma_send.at[dst], ma_recv.at[dst], device))

    index_a(0, NX, pair_at(1, 0))
    for r in (1, 2, NZ - 2, NZ - 1):
        index_z(0, r, r)
    for r in range(1, NX):
        index_a(0, r, x_at(r))

    forward(0, 1, 0)

    @pl.when(core == 1)
    def _():
        for c in cross_a:
            c.wait_recv()
        for c in xs[:4]:
            c.start()

    sent.extend(xs[:4])
    go(ts[0])
    forward(0, 1, 1)
    on_z[2].wait_recv()
    index_z(2, 4, 2)
    on_z[1].wait_recv()
    index_z(1, 3, 2)
    on_z[NZ - 1].wait_recv()
    index_z(NZ - 1, 5, NZ - 2)
    on_a[NX].wait_recv()
    for r in range(1, NX):
        index_a(NX, NX + r, x_at(r))
    forward(1, 1, 0)

    forward(0, 2, 0)
    forward(0, 2, 1)
    forward(1, 2, 0)
    for c in [on_z[r] for r in (3, 4, 5, 6)] + [on_a[r] for r in (1, 2, 3, 5, 6, 7)]:
        c.wait_recv()
    b_cols = jnp.concatenate([meta_b[(NZ - d) % NZ, 1:2, :] for d in range(NZ)], axis=0)
    away = (lane // 32 - x + NX) % NX
    inside = lane % 32
    place = jnp.where(away == 0, 0, jnp.where(away == 3, 1, jnp.where(away == 1, 2, 3))) * SPAN + inside
    owner = jnp.zeros((8, 128), jnp.int32)
    for m in range(1, ROWS):
        owner = owner + jnp.where(inside >= SLOTS * m, 1, 0)
    group = (y_lo * NZ + (line + z) % NZ) * 4 + rep

    def pick(where, value):
        return jnp.sum(jnp.where(where, value, 0), axis=1, keepdims=True)

    for s in range(2):
        flip = (core + s) % 2
        base = flip * NX
        codes = meta_a[base, 0:1, :]
        for rx in range(1, NX):
            codes = codes + meta_a[base + rx, 0:1, :]
        codes = jnp.broadcast_to(codes, (8, 128)) - 1
        wanted = jnp.broadcast_to(meta_a[base, 2:3, :], (8, 128))
        match = (codes >= 0) & (codes // 8 == group)
        first = jnp.min(jnp.where(match, lane, 1000), axis=1, keepdims=True)
        last = jnp.max(jnp.where(match, lane, -1), axis=1, keepdims=True)
        result = jnp.zeros((8, 128), jnp.int32)
        for k in range(2):
            chosen = match & (lane == first) if k == 0 else match & (lane == last) & (lane != first)
            exists = pick(chosen, 1)
            index = pick(chosen, place + s * NX * SPAN)
            offset = pick(chosen, codes % 8)
            row = pick(chosen, owner)
            result = result + jnp.where(lane == k * 32, index, 0)
            result = result + jnp.where(lane == k * 32 + 1, offset * TERMS, 0)
            result = result + jnp.where(lane == k * 32 + 2, row, 0)
            kept = [pick(lane == row * KEPT + q, wanted) for q in range(KEPT)]
            for t in range(TERMS):
                target = pick(lane == offset * TERMS + t, b_cols)
                for q in range(KEPT):
                    hit = jnp.where((target == kept[q]) & (exists > 0), 1, 0)
                    result = result + jnp.where(lane == k * 32 + 8 + t * KEPT + q, hit, 0)
        table_v[s] = result
    to_scalar = pltpu.make_async_copy(table_v, table_s, tab_sem)
    to_scalar.start()
    to_scalar.wait()

    xs[0].wait_recv()
    go(xs[4])
    xs[1].wait_recv()
    go(xs[5])
    begin(2)
    forward(0, 3, 0)
    forward(0, 3, 1, False)
    xs[2].wait_recv()
    go(ts[1])
    xs[3].wait_recv()
    go(ts[2])

    def multiply(h, ds, stream):
        lo = (y_lo + core + stream) % 2
        base = lo * 2 * ROWS if h == 0 else ((h - 1) * 2 + lo) * ROWS
        into = acc if h == 0 else quarter_acc
        slots = [(d, k) for d in ds for k in range(2)]
        for d, k in slots:
            buf = bufs[h][d]
            a = a_all[table_s[stream, d, k * 32]]
            offset = table_s[stream, d, k * 32 + 1]
            terms = [buf[offset + t] for t in range(TERMS)]
            chosen = []
            for q in range(KEPT):
                weights = [table_s[stream, d, k * 32 + 8 + t * KEPT + q].astype(jnp.float32) for t in range(TERMS)]
                chosen.append(weights[0] * terms[0] + weights[1] * terms[1] + weights[2] * terms[2])
            turned = [pltpu.roll(c, 64, 1) for c in chosen]
            if h == 0:
                b = jnp.concatenate([
                    jnp.concatenate([jnp.where(left, chosen[g], turned[g + 2]) for g in range(2)], axis=1),
                    jnp.concatenate([jnp.where(left, turned[g], chosen[g + 2]) for g in range(2)], axis=1),
                ], axis=0)
            else:
                parts = []
                for upper in (True, False):
                    pair = [
                        jnp.where(left_thin, chosen[g], turned[g + 1]) if upper
                        else jnp.where(left_thin, turned[g], chosen[g + 1])
                        for g in (0, 2)
                    ]
                    parts.append(jnp.where(even, pair[0], pltpu.roll(pair[1], 32, 1)))
                    parts.append(jnp.where(even, pltpu.roll(pair[0], 96, 1), pair[1]))
                b = jnp.concatenate(parts, axis=0)
            a_hi = a.astype(jnp.bfloat16)
            a_lo = (a - a_hi.astype(jnp.float32)).astype(jnp.bfloat16)
            b_hi = b.astype(jnp.bfloat16)
            b_lo = (b - b_hi.astype(jnp.float32)).astype(jnp.bfloat16)
            dot = functools.partial(jnp.dot, preferred_element_type=jnp.float32)
            prod[slots.index((d, k)), :, pl.ds(0, b.shape[1])] = dot(a_hi, b_hi) + (dot(a_hi, b_lo) + dot(a_lo, b_hi))
        rows = [table_s[stream, d, k * 32 + 2] for d, k in slots]

        def update(i, carry):
            weights = [jnp.where(row == i, 1.0, 0.0).astype(jnp.float32) for row in rows]
            for g in range(2 if h == 0 else 1):
                where = base + g * ROWS + i
                total = None if 0 in ds else into[where]
                for n, weight in enumerate(weights):
                    term = weight * prod[n, :, pl.ds(g * 128, 128)]
                    total = term if total is None else total + term
                into[where] = total
            return carry

        lax.fori_loop(0, ROWS, update, 0)

    def multiply_all(h, *ds):
        def both(stream, carry):
            multiply(h, ds, stream)
            return carry

        lax.fori_loop(0, 2, both, 0)

    cores, far, near = {}, {}, {}

    def to_sibling(h, e):
        lo = (y_lo + e) % 2
        if h == 0:
            src = acc.at[pl.ds((lo * 2 + 1 - core) * ROWS, ROWS)]
        else:
            for i in range(ROWS):
                halves = to_halves(quarter_acc[((h - 1) * 2 + lo) * ROWS + i])
                for c in range(2):
                    own_core[(((h - 1) * 2 + lo) * 2 + c) * ROWS + i] = halves[c]
            src = own_core.at[pl.ds((((h - 1) * 2 + lo) * 2 + 1 - core) * ROWS, ROWS)]
        cores[h, e] = go(copy(
            src, core_in[h].at[pl.ds(e * ROWS, ROWS)], c_send.at[h * 2 + e], c_recv.at[h * 2 + e], sibling,
        ))

    def fold(h, e):
        cores[h, e].wait_recv()
        lo = (y_lo + e) % 2
        for i in range(ROWS):
            if h == 0:
                pieces = to_halves(core_in[h][e * ROWS + i] + acc[(lo * 2 + core) * ROWS + i])
            else:
                pieces = to_quarters(
                    core_in[h][e * ROWS + i] + own_core[(((h - 1) * 2 + lo) * 2 + core) * ROWS + i]
                )
            packed[h][lo * ROWS + i] = pieces[0]
            packed[h][(2 + lo) * ROWS + i] = pieces[1]

    def place_of(h, step):
        return ((y + step) % 4) * ROWS

    def send_y(h, step, lo, dst, dst_lo, index, way):
        return go(copy(
            packed[h].at[pl.ds(place_of(h, step) + lo, MID)], dst.at[pl.ds(dst_lo, MID)],
            r_send.at[h * 6 + index], r_recv.at[h * 6 + index], y_at(way),
        ))

    def fold_far(h):
        fold(h, 0)
        far[h] = [
            send_y(h, 2, 0, far_in[h], 0, 0, 1),
            send_y(h, 2, MID, far_in[h], MID, 1, 3),
        ]

    def fold_near(h):
        fold(h, 1)
        near[h] = [
            send_y(h, 1, MID, near_in[h], MID, 2, 1),
            send_y(h, 3, 0, near_in[h], ROWS, 3, 3),
        ]

    def add_far(h):
        for way, lo in ((1, 0), (3, MID)):
            far[h][lo // MID].wait_recv()
            for i in range(lo, lo + MID):
                where = place_of(h, way) + i
                packed[h][where] = packed[h][where] + far_in[h][i]
            near[h].append(send_y(
                h, way, lo, near_in[h], (0 if way == 1 else ROWS) + lo, 4 + lo // MID, way,
            ))

    def finish(h):
        for c in near[h]:
            c.wait_recv()
        for i in range(ROWS):
            where = place_of(h, 0) + i
            packed[h][where] = packed[h][where] + near_in[h][i] + near_in[h][ROWS + i]

    def last(h):
        hops[h, 1, 3, 0].wait_recv()
        hops[h, -1, 3, 0].wait_recv()

    xs[4].wait_recv()
    xs[5].wait_recv()
    go(ts[3])
    forward(1, 3, 0)
    for c in ts:
        c.wait_recv()
    multiply_all(0, 0, 1, 7)
    multiply_all(0, 2, 6)
    forward(2, 1, 0)
    multiply_all(1, 0, 1, 7)
    multiply_all(1, 2, 6)
    forward(2, 1, 1)
    last(0)
    multiply_all(0, 3, 5, 4)
    to_sibling(0, 0)
    to_sibling(0, 1)
    last(1)
    multiply_all(1, 3, 5, 4)
    to_sibling(1, 0)
    to_sibling(1, 1)
    forward(2, 2, 0)
    fold_far(0)
    fold_far(1)
    fold_near(0)
    fold_near(1)
    forward(2, 2, 1)
    multiply_all(2, 0, 1, 7)
    add_far(0)
    add_far(1)
    forward(2, 3, 0)
    multiply_all(2, 2, 6)
    forward(2, 3, 1, False)
    multiply_all(2, 3, 5)
    last(2)
    multiply(2, (4,), core)
    to_sibling(2, 0)
    multiply(2, (4,), 1 - core)
    to_sibling(2, 1)
    finish(0)
    finish(1)
    fold_far(2)
    fold_near(2)
    add_far(2)
    finish(2)
    for i in range(ROWS):
        where = place_of(0, 0) + i
        first, third, fourth = packed[0][where], packed[1][where], packed[2][where]
        second = jnp.concatenate([
            jnp.where(even, third, pltpu.roll(fourth, 32, 1)),
            jnp.where(even, pltpu.roll(third, 96, 1), fourth),
        ], axis=0)
        out_ref[i, pl.ds(0, 64)] = jnp.where(left, first, pltpu.roll(second, 64, 1))
        out_ref[i, pl.ds(64, 64)] = jnp.where(left, pltpu.roll(first, 64, 1), second)

    for c in sent:
        c.wait_send()

    @pl.when(core == 1)
    def _():
        for c in cross_a:
            c.wait_send()


def local(a_vals, a_group, a_offset, b_vals, b_cols, c_cols):
    a = a_vals.reshape(-1, 128, 128)
    b = b_vals.reshape(-1, 128, 128)
    blocks = lambda n: pltpu.VMEM((n, 128, 128), jnp.float32)
    thin = lambda n: pltpu.VMEM((n, 64, 128), jnp.float32)
    slim = lambda n: pltpu.VMEM((n, 32, 128), jnp.float32)
    dma = lambda n: pltpu.SemaphoreType.DMA((n,))
    out = pl.pallas_call(
        kernel,
        out_shape=jax.ShapeDtypeStruct((ROWS, 128, 128), jnp.float32),
        in_specs=[pl.BlockSpec(memory_space=pltpu.SMEM)] * 4 + [pl.BlockSpec(memory_space=pltpu.HBM)] * 2,
        out_specs=pl.BlockSpec(memory_space=pltpu.VMEM),
        scratch_shapes=[thin(BLOCKS)] * NZ + [slim(BLOCKS)] * (2 * NZ) + [
            blocks(BLOCKS),
            blocks(2 * NX * SPAN),
            pltpu.VMEM((8, 128, 256), jnp.float32),
            blocks(4 * ROWS), thin(8 * ROWS),
            blocks(2 * ROWS), thin(2 * ROWS), thin(2 * ROWS),
            blocks(4 * ROWS),
            thin(4 * ROWS), slim(4 * ROWS), slim(4 * ROWS),
            thin(ROWS), slim(ROWS), slim(ROWS),
            thin(2 * ROWS), slim(2 * ROWS), slim(2 * ROWS),
            pltpu.VMEM((8, 8, 128), jnp.int32),
            pltpu.VMEM((8, 8, 128), jnp.int32),
            pltpu.VMEM((2, 8, 128), jnp.int32),
            pltpu.SMEM((2, 8, 128), jnp.int32),
            dma(2), pltpu.SemaphoreType.DMA,
            dma(8), dma(8), dma(8), dma(8),
            dma(24), dma(24), dma(24), dma(24),
            dma(2), dma(2), dma(6), dma(6), dma(4), dma(4),
            dma(6), dma(6), dma(18), dma(18),
        ],
        compiler_params=pltpu.CompilerParams(
            collective_id=0, has_side_effects=True, vmem_limit_bytes=62 * 1024 * 1024
        ),
        cost_estimate=pl.CostEstimate(flops=2 * 10 ** 9, bytes_accessed=3 * 10 ** 6, transcendentals=0),
    )(
        a_group.transpose(1, 2, 0), a_offset.T, b_cols.transpose(2, 1, 0), c_cols[:, 0].T, a, b,
    )
    return out.reshape(ROWS, 1, 1, 128, 128)


def solution(mesh):
    placed = (
        P("col", "row", None, None),
        P("col", "row", None),
        P("col", "row"),
        P(("col", "rep"), "row", None, None, None),
        P(("col", "rep"), "row", None),
        P("col", "row", None),
    )
    return jax.shard_map(
        local,
        mesh=mesh,
        in_specs=placed,
        out_specs=P("col", "row", "rep", None, None),
        check_vma=False,
    )
```
